512 devices in a mesh: dp: 32 (over z, core), bal: 16 (over y, x).
Axes of the slice: x: 4, y: 4, z: 16, core: 2. Of those that a mesh axis runs over, the one named last changes fastest.
Arguments:
- tiles: bfloat16 [11776, 270, 256], P(('dp', 'bal')), may hold values from -6 to 6
- cotangent: bfloat16 [11776, 32, 256], P(('dp', 'bal')), may hold values from -6 to 6
- halo_flags: int32 [11776, 3], P(('dp', 'bal')), may hold values 0 or 1
- send_plan: int32 [512, 16, 2], P(('dp', 'bal')), may hold values from -1 to 22, as said below
- spatial_weight: bfloat16 [2304, 256], P('bal'), may hold values from -0.125 to 0.125
- temporal_weight: bfloat16 [512, 256], P('bal'), may hold values from -0.25 to 0.25
Outputs:
- features: bfloat16 [11776, 32, 256], P(('dp', 'bal'))
- spatial_grad: float32 [2304, 256], P('bal', 'dp')
- temporal_grad: float32 [512, 256], P('bal', 'dp')
The draws below stay inside these ranges and needn't reach their ends.
Inputs may be any that keep to these rules, and one draw needn't show every extreme that they name: `send_plan`: row g lists, for each worker w of owner g's bal group (bal index w, same dp index) and each pair slot q, the owner's tile slot sent there, or -1. The live slots of an owner are its slots 0 to n - 1, each named exactly once, with n from 1 to 23; in every group some owner has exactly 23. One owner sends at most 2 tiles to one worker, and some pair holds exactly 2; every worker receives exactly 12 tiles.
All inputs are finite; a program needn't handle non-finite values. No bound on the sum of `halo_flags` on one device may be relied on, other than what follows from the above.
Results may differ from the reference program's by a relative error of at most 0.0049.
Values may be sent and summed in bfloat16 or wider, within the bound.
No kernel may reach another device: no remote copies, remote signals or barrier semaphores. Data moves between devices by JAX's collectives and lax.ppermute only.
A program may use at most 128 MiB of HBM per device.

```python
import jax
import jax.numpy as jnp
from jax import lax

C = 256
TILE_ROWS = 2
TILE_COLUMNS = 4
OUTPUT_FRAMES = 4
TEMPORAL_DILATION = 2
WORK_TILES = 12
OWNED = 23
CAPACITY = 2
IN_FR = 6
IN_H = 5
IN_W = 9
IN_PIX = 270
OUT_PIX = 32
OWN_SLOTS = 11776
N_DP = 32
N_BAL = 16


def group_table(key):
    key_pairs, key_owner, key_worker = jax.random.split(key, 3)
    tile_total = N_BAL * WORK_TILES
    imbalance = jax.random.randint(key_pairs, (N_BAL // 2,), 0, WORK_TILES)
    imbalance = imbalance.at[0].set(WORK_TILES - 1)
    ordered = jnp.stack([WORK_TILES + imbalance, WORK_TILES - imbalance], axis=1).reshape(N_BAL)
    owner_order = jax.random.permutation(key_owner, N_BAL)
    tile_counts = jnp.zeros((N_BAL,), jnp.int32).at[owner_order].set(ordered.astype(jnp.int32))
    range_ends = jnp.cumsum(tile_counts)
    range_starts = range_ends - tile_counts
    tile_ids = jnp.arange(tile_total, dtype=jnp.int32)
    owner_ids = jnp.sum((range_ends[None, :] <= tile_ids[:, None]).astype(jnp.int32), axis=1)
    slot_ids = tile_ids - range_starts[owner_ids]
    block_ids = tile_ids // CAPACITY
    worker_order = jax.random.permutation(key_worker, N_BAL).astype(jnp.int32)
    worker_ids = worker_order[block_ids % N_BAL]
    same_pair = (owner_ids[:, None] == owner_ids[None, :]) & (worker_ids[:, None] == worker_ids[None, :]) & (tile_ids[None, :] < tile_ids[:, None])
    pair_rank = jnp.sum(same_pair.astype(jnp.int32), axis=1)
    send_table = jnp.full((N_BAL, N_BAL, CAPACITY), -1, jnp.int32)
    return send_table.at[owner_ids, worker_ids, pair_rank].set(slot_ids)


def draw_send_plan(key, part):
    base_key = jax.random.fold_in(key, 11)
    key_list = jax.random.split(base_key, N_DP)
    tables = jax.vmap(group_table)(key_list)
    return tables.reshape(N_DP * N_BAL, N_BAL, CAPACITY)


def plant(array, key, low, top_value):
    shape = array.shape
    spot = [jax.random.randint(jax.random.fold_in(key, axis), (), 0, shape[axis]) for axis in range(len(shape))]
    array = array.at[tuple(spot)].set(low)
    longest = shape.index(max(shape))
    spot[longest] = (spot[longest] + 1) % shape[longest]
    return array.at[tuple(spot)].set(top_value)


def levels(key, shape, cuts, smallest, largest):
    level = 1.0
    for position, blocks in cuts:
        draws = jax.random.uniform(jax.random.fold_in(jax.random.fold_in(key, 6), position), (blocks,), jnp.float32, smallest / len(cuts), largest / len(cuts))
        level = level * jnp.repeat(jnp.exp(draws), shape[position] // blocks).reshape((-1,) + (1,) * (len(shape) - 1 - position))
    return level


def gaussian(key, extent, width, limit, cuts=(), held_as=jnp.bfloat16):
    entries = width * jax.random.normal(key, extent, jnp.float32)
    if cuts:
        entries = entries * levels(key, extent, cuts, -0.22, 0.18)
    return jnp.clip(entries, -limit, limit).astype(held_as)


def setup_inputs(seed: int = 0) -> dict:
    seeds = jax.random.split(jax.random.key(seed), 7)
    tiles = gaussian(seeds[0], (OWN_SLOTS, IN_PIX, C), 1.0, 6.0, ((0, 512),))
    cotangent = gaussian(seeds[1], (OWN_SLOTS, OUT_PIX, C), 1.0, 6.0, ((0, 512),))
    halo_flags = plant((jax.random.randint(seeds[2], (OWN_SLOTS, 3), 0, 2) < 1).astype(jnp.int32), jax.random.fold_in(seeds[2], 1), 0, 1)
    send_plan = draw_send_plan(jax.random.fold_in(seeds[6], 71), 0)
    spatial_weight = gaussian(seeds[4], (9 * C, C), (9 * C) ** -0.5, 0.125, ((0, 16),))
    temporal_weight = gaussian(seeds[5], (2 * C, C), (2 * C) ** -0.5, 0.25, ((0, 16),))
    return dict(tiles=tiles, cotangent=cotangent, halo_flags=halo_flags, send_plan=send_plan, spatial_weight=spatial_weight, temporal_weight=temporal_weight)


def keep_mask(halo_flag_row):
    frame_indices = jnp.arange(IN_FR)[:, None, None]
    row_ids = jnp.arange(IN_H)[None, :, None]
    col_ids = jnp.arange(IN_W)[None, None, :]
    top_ok = (row_ids > 0) | (halo_flag_row[0] > 0)
    left_ok = (col_ids > 0) | (halo_flag_row[1] > 0)
    past_frame_valid = (frame_indices >= TEMPORAL_DILATION) | (halo_flag_row[2] > 0)
    return top_ok & left_ok & past_frame_valid

def tile_pass(inputs, cotang, spatial_full, temporal_full):
    tile_number = inputs.shape[0]
    channel_index = inputs.shape[-1]
    tap_list = []
    for row_tap in range(3):
        for col_tap in range(3):
            tap_list.append(inputs[:, :, row_tap:row_tap + 2 * TILE_ROWS - 1:2, col_tap:col_tap + 2 * TILE_COLUMNS - 1:2, :])
    patches = jnp.concatenate(tap_list, axis=-1).reshape(-1, 9 * channel_index)
    pre_act = jnp.dot(patches, spatial_full, preferred_element_type=jnp.float32)
    activation = jax.nn.silu(pre_act).astype(jnp.bfloat16).reshape(tile_number, IN_FR, TILE_ROWS * TILE_COLUMNS, channel_index)
    paired_tiles = jnp.concatenate([activation[:, TEMPORAL_DILATION:], activation[:, :OUTPUT_FRAMES]], axis=-1).reshape(-1, 2 * channel_index)
    outputs = jnp.dot(paired_tiles, temporal_full, preferred_element_type=jnp.float32).astype(jnp.bfloat16)
    grad_out = cotang.reshape(-1, channel_index)
    grad_temp = lax.dot_general(paired_tiles, grad_out, (((0,), (0,)), ((), ())), preferred_element_type=jnp.float32)
    grad_pair = lax.dot_general(grad_out, temporal_full, (((1,), (1,)), ((), ())), preferred_element_type=jnp.float32)
    grad_pair = grad_pair.reshape(tile_number, OUTPUT_FRAMES, TILE_ROWS * TILE_COLUMNS, 2 * channel_index)
    causal_padding = jnp.zeros((tile_number, TEMPORAL_DILATION, TILE_ROWS * TILE_COLUMNS, channel_index), jnp.float32)
    grad_activ = jnp.concatenate([causal_padding, grad_pair[..., :channel_index]], axis=1) + jnp.concatenate([grad_pair[..., channel_index:], causal_padding], axis=1)
    pre_view = pre_act.reshape(grad_activ.shape)
    sigmoid_v = jax.nn.sigmoid(pre_view)
    grad_pre = (grad_activ * sigmoid_v * (1.0 + pre_view * (1.0 - sigmoid_v))).astype(jnp.bfloat16).reshape(-1, channel_index)
    grad_space = lax.dot_general(patches, grad_pre, (((0,), (0,)), ((), ())), preferred_element_type=jnp.float32)
    return (outputs.reshape(tile_number, OUT_PIX, channel_index), grad_space, grad_temp)

def reference(tiles, cotangent, halo_flags, send_plan, spatial_weight, temporal_weight):
    device_count = N_DP * N_BAL
    slot_ids = jnp.arange(OWNED, dtype=jnp.int32)
    plan_rows = send_plan.reshape(device_count, N_BAL * CAPACITY)
    live_all = jnp.any(plan_rows[:, :, None] == slot_ids[None, None, :], axis=1).reshape(-1)
    tile_view = tiles.reshape(OWN_SLOTS, IN_FR, IN_H, IN_W, C)
    cot_view = cotangent.reshape(OWN_SLOTS, OUTPUT_FRAMES, TILE_ROWS, TILE_COLUMNS, C)

    def one_tile(carry, item):
        tile_one, cot_one, flag_one, live_one = item

        def run_tile(sums):
            masked = jnp.where(keep_mask(flag_one)[..., None], tile_one, jnp.zeros_like(tile_one))
            outputs, grad_space, grad_temp = tile_pass(masked[None], cot_one[None], spatial_weight, temporal_weight)
            return (outputs[0], sums[0] + grad_space, sums[1] + grad_temp)

        def skip_tile(sums):
            return (jnp.zeros((OUT_PIX, C), jnp.bfloat16), sums[0], sums[1])
        outputs, sum_space, sum_temp = lax.cond(live_one, run_tile, skip_tile, carry)
        return ((sum_space, sum_temp), outputs)
    start = (jnp.zeros((9 * C, C), jnp.float32), jnp.zeros((2 * C, C), jnp.float32))
    (sum_space, sum_temp), features = lax.scan(one_tile, start, (tile_view, cot_view, halo_flags, live_all))
    factor = 1.0 / jnp.sqrt(jnp.float32(N_DP * N_BAL * WORK_TILES))
    return (features, sum_space * factor, sum_temp * factor)
```

```python
import functools
import math

import jax
import jax.numpy as jnp
from jax import lax
from jax.experimental import pallas as pl
from jax.experimental.pallas import tpu as pltpu
from jax.sharding import PartitionSpec as P

C = 256
OWNED = 23
IN_PIX = 270
OUT_PIX = 32
ACT_PIX = 48
TAPS = 9
WORK_TILES = 12
GROUP = 8
STEPS = 3
PAD_TILES = GROUP * STEPS
ROWS = PAD_TILES * ACT_PIX
GROUP_ROWS = GROUP * ACT_PIX
COT_ROWS = PAD_TILES * OUT_PIX
GROUP_COT = GROUP * OUT_PIX
WINDOWS = ((0, 128), (80, 128), (160, 110))
PAIR_ROWS = 16 * TAPS
BF = jnp.bfloat16
F32 = jnp.float32


def selection():
    row = lax.broadcasted_iota(jnp.int32, (3, PAIR_ROWS, 128), 1)
    col = lax.broadcasted_iota(jnp.int32, (3, PAIR_ROWS, 128), 2)
    group = lax.broadcasted_iota(jnp.int32, (3, PAIR_ROWS, 128), 0)
    tap, cell = row // 16, row % 16
    frame, i, j = cell // 8, (cell // 4) % 2, cell % 4
    source = (2 * group + frame) * 45 + (2 * i + tap // 3) * 9 + 2 * j + tap % 3
    pick = (source == col + 80 * group).astype(BF)
    kind = lax.broadcasted_iota(jnp.int32, (3, 8, 128), 1)
    cell = lax.broadcasted_iota(jnp.int32, (3, 8, 128), 2) + 80 * lax.broadcasted_iota(
        jnp.int32, (3, 8, 128), 0
    )
    top = (kind == 0) & (cell % 45 < 9)
    left = (kind == 1) & (cell % 9 == 0)
    past = (kind == 2) & (cell < 90)
    return pick, (top | left | past).astype(F32)


def live_count(plan_ref):
    count = plan_ref[0, 0]
    for q in range(2):
        for w in range(16):
            count = jnp.maximum(count, plan_ref[q, w])
    return count + 1


def patch_kernel(flags_ref, plan_ref, tiles_ref, cot_ref, pick_ref, mark_ref, perm_ref,
                 patch_ref, patcht_ref, cotl_ref, cotp_ref):
    step = pl.program_id(0)
    count = live_count(plan_ref)
    for t in range(GROUP):
        slot = step * GROUP + t
        rows = slice(t * ACT_PIX, (t + 1) * ACT_PIX)

        @pl.when(slot < OWNED)
        def _():
            flag = jnp.minimum(slot, OWNED - 1)
            off = [jnp.where(flags_ref[k, flag] > 0, 0.0, 1.0) for k in range(3)]
            for g, (first, size) in enumerate(WINDOWS):
                marks = mark_ref[g]
                out = marks[0:1] * off[0] + marks[1:2] * off[1] + marks[2:3] * off[2]
                keep = jnp.where(out > 0.0, 0.0, 1.0).astype(BF)
                chosen = (pick_ref[g] * keep)[:, :size]
                got = jnp.dot(chosen, tiles_ref[t, first:first + size, :],
                              preferred_element_type=F32).astype(BF)
                for tap in range(TAPS):
                    patch_ref[t * ACT_PIX + 16 * g:t * ACT_PIX + 16 * (g + 1),
                              tap * C:(tap + 1) * C] = got[tap * 16:(tap + 1) * 16]

        @pl.when(slot >= OWNED)
        def _():
            patch_ref[rows, :] = jnp.zeros((ACT_PIX, TAPS * C), BF)

        cells = slice(t * OUT_PIX, (t + 1) * OUT_PIX)
        cot = jnp.where(slot < count, cot_ref[t].astype(F32), 0.0).astype(BF)
        cotl_ref[cells, :] = cot
        cotp_ref[cells, :] = jnp.dot(cot, perm_ref[...], preferred_element_type=F32).astype(BF)
    for tap in range(TAPS):
        patcht_ref[tap * C:(tap + 1) * C, :] = patch_ref[:, tap * C:(tap + 1) * C].T


def main_kernel(plan_ref, weights_ref, cotl_ref, cotp_ref, perm_ref, patch_hbm, patcht_hbm,
                feat_ref, keep_ref, send_ref,
                patch_s, patcht_s, spatial_s, temporal_s, pair_s, gpre_s, sems):
    copies = [
        pltpu.make_async_copy(patch_hbm.at[pl.ds(g * GROUP_ROWS, GROUP_ROWS), :],
                              patch_s.at[pl.ds(g * GROUP_ROWS, GROUP_ROWS), :], sems.at[g])
        for g in range(STEPS)
    ]
    copies.append(pltpu.make_async_copy(patcht_hbm, patcht_s, sems.at[STEPS]))
    for copy in copies:
        copy.start()
    count = live_count(plan_ref)
    for b in range(16):
        spatial_s[b * 144:(b + 1) * 144, :] = weights_ref[b, :144, :]
        temporal_s[b * 32:(b + 1) * 32, :] = weights_ref[b, 144:, :]
    for g in range(STEPS):
        copies[g].wait()
        rows = slice(g * GROUP_ROWS, (g + 1) * GROUP_ROWS)
        cells = slice(g * GROUP_COT, (g + 1) * GROUP_COT)
        pre = jnp.dot(patch_s[rows, :], spatial_s[...], preferred_element_type=F32)
        sig = 1.0 / (1.0 + jnp.exp(-pre))
        act = (pre * sig).astype(BF)
        slope = sig * (1.0 + pre * (1.0 - sig))
        for t in range(GROUP):
            out = slice(g * GROUP_COT + t * OUT_PIX, g * GROUP_COT + (t + 1) * OUT_PIX)
            pair_s[out, :C] = act[t * ACT_PIX + 16:(t + 1) * ACT_PIX]
            pair_s[out, C:] = act[t * ACT_PIX:t * ACT_PIX + OUT_PIX]
        gpair = lax.dot_general(cotl_ref[cells, :], temporal_s[...], (((1,), (1,)), ((), ())),
                                preferred_element_type=F32)
        pieces = []
        for t in range(GROUP):
            a, b, c = t * OUT_PIX, t * OUT_PIX + 16, (t + 1) * OUT_PIX
            pieces.append(gpair[a:b, C:])
            pieces.append(gpair[a:b, :C] + gpair[b:c, C:])
            pieces.append(gpair[b:c, :C])
        gact = jnp.concatenate(pieces, axis=0)
        gpre = (gact * slope).astype(BF)
        gpre_s[rows, :] = jnp.dot(gpre, perm_ref[...], preferred_element_type=F32).astype(BF)
        feat = jnp.dot(pair_s[cells, :], temporal_s[...], preferred_element_type=F32).astype(BF)
        for t in range(GROUP):
            slot = g * GROUP + t
            if slot < OWNED:
                one = feat[t * OUT_PIX:(t + 1) * OUT_PIX]
                feat_ref[slot] = jnp.where(slot < count, one, jnp.zeros_like(one))

    def put(first, grad):
        last = first + grad.shape[0]
        for b in range(first // 144, (last - 1) // 144 + 1):
            lo, hi = max(first, 144 * b), min(last, 144 * (b + 1))
            piece = grad[lo - first:hi - first]
            keep_ref[b, lo - 144 * b:hi - 144 * b, :] = piece[:, :128]
            send_ref[b, lo - 144 * b:hi - 144 * b, :] = piece[:, 128:].astype(BF)

    temporal = lax.dot_general(pair_s[...], cotp_ref[...], (((0,), (0,)), ((), ())),
                               preferred_element_type=F32)
    for b in range(16):
        piece = temporal[b * 32:(b + 1) * 32]
        keep_ref[b, 144:, :] = piece[:, :128]
        send_ref[b, 144:, :] = piece[:, 128:].astype(BF)
    copies[STEPS].wait()
    for tap in range(TAPS):
        put(tap * C, jnp.dot(patcht_s[tap * C:(tap + 1) * C, :], gpre_s[...],
                             preferred_element_type=F32))


def per_device(tiles, cotangent, halo_flags, send_plan, spatial_weight, temporal_weight):
    core = lax.axis_index("dp") % 2
    mine = jnp.concatenate([spatial_weight, temporal_weight], axis=0)
    blocks = jnp.broadcast_to(mine[None], (16,) + mine.shape)
    weights = lax.all_to_all(blocks, "bal", 0, 0)

    pick, marks = selection()
    row = lax.broadcasted_iota(jnp.int32, (C, C), 0)
    col = lax.broadcasted_iota(jnp.int32, (C, C), 1)
    wanted = ((col % 128) // 8) * 16 + jnp.bitwise_xor(core, col // 128) * 8 + col % 8
    perm = (row == wanted).astype(BF)
    flags = halo_flags.T
    plan = send_plan[0].T

    whole = lambda shape: pl.BlockSpec(shape, lambda s: (0,) * len(shape))
    smem = pl.BlockSpec(memory_space=pltpu.SMEM)
    patches, patches_t, cot_live, cot_perm = pl.pallas_call(
        patch_kernel,
        grid=(STEPS,),
        in_specs=[
            smem, smem,
            pl.BlockSpec((GROUP, IN_PIX, C), lambda s: (s, 0, 0)),
            pl.BlockSpec((GROUP, OUT_PIX, C), lambda s: (s, 0, 0)),
            whole((3, PAIR_ROWS, 128)), whole((3, 8, 128)), whole((C, C)),
        ],
        out_specs=[
            pl.BlockSpec((GROUP_ROWS, TAPS * C), lambda s: (s, 0)),
            pl.BlockSpec((TAPS * C, GROUP_ROWS), lambda s: (0, s)),
            pl.BlockSpec((GROUP_COT, C), lambda s: (s, 0)),
            pl.BlockSpec((GROUP_COT, C), lambda s: (s, 0)),
        ],
        out_shape=[
            jax.ShapeDtypeStruct((ROWS, TAPS * C), BF),
            jax.ShapeDtypeStruct((TAPS * C, ROWS), BF),
            jax.ShapeDtypeStruct((COT_ROWS, C), BF),
            jax.ShapeDtypeStruct((COT_ROWS, C), BF),
        ],
        compiler_params=pltpu.CompilerParams(vmem_limit_bytes=40 * 2**20),
        cost_estimate=pl.CostEstimate(flops=6 * 10**9, bytes_accessed=15 * 10**6, transcendentals=0),
        name="patches",
    )(flags, plan, tiles, cotangent, pick, marks, perm)

    vmem = pl.BlockSpec(memory_space=pltpu.VMEM)
    hbm = pl.BlockSpec(memory_space=pl.ANY)
    features, keep, send = pl.pallas_call(
        main_kernel,
        in_specs=[smem, vmem, vmem, vmem, vmem, hbm, hbm],
        out_specs=[vmem, vmem, vmem],
        out_shape=[
            jax.ShapeDtypeStruct((OWNED, OUT_PIX, C), BF),
            jax.ShapeDtypeStruct((16, 176, 128), F32),
            jax.ShapeDtypeStruct((16, 176, 128), BF),
        ],
        scratch_shapes=[
            pltpu.VMEM((ROWS, TAPS * C), BF),
            pltpu.VMEM((TAPS * C, ROWS), BF),
            pltpu.VMEM((TAPS * C, C), BF),
            pltpu.VMEM((2 * C, C), BF),
            pltpu.VMEM((COT_ROWS, 2 * C), BF),
            pltpu.VMEM((ROWS, C), BF),
            pltpu.SemaphoreType.DMA((STEPS + 1,)),
        ],
        compiler_params=pltpu.CompilerParams(vmem_limit_bytes=48 * 2**20),
        cost_estimate=pl.CostEstimate(flops=4 * 10**9, bytes_accessed=15 * 10**6, transcendentals=0),
        name="section",
    )(plan, weights, cot_live, cot_perm, perm, patches, patches_t)

    other = lax.ppermute(send, "dp", [(i, i ^ 1) for i in range(32)])
    chip = (keep + other.astype(F32)).astype(BF)
    part = lax.all_to_all(chip, "bal", 0, 0)
    part = jnp.sum(part.astype(F32), axis=0)
    part = part.T.reshape(16, 8, 176)
    along_z = [[2 * z + c for z in range(16)] for c in range(2)]
    last = lax.all_to_all(part, "dp", 0, 0, axis_index_groups=along_z)
    factor = 1.0 / math.sqrt(lax.axis_size("dp") * lax.axis_size("bal") * WORK_TILES)
    total = jnp.sum(last, axis=0) * factor
    return features, total[:, :144].T, total[:, 144:].T


def solution(mesh):
    in_specs = (
        P(("dp", "bal"), None, None),
        P(("dp", "bal"), None, None),
        P(("dp", "bal"), None),
        P(("dp", "bal"), None, None),
        P("bal", None),
        P("bal", None),
    )
    out_specs = (P(("dp", "bal"), None, None), P("bal", "dp"), P("bal", "dp"))
    return jax.shard_map(
        per_device, mesh=mesh, in_specs=in_specs, out_specs=out_specs, check_vma=False
    )
```

```python
import functools
import math

import jax
import jax.numpy as jnp
from jax import lax
from jax.experimental import pallas as pl
from jax.experimental.pallas import tpu as pltpu
from jax.sharding import PartitionSpec as P

C = 256
OWNED = 23
IN_PIX = 270
OUT_PIX = 32
ACT_PIX = 48
TAPS = 9
WORK_TILES = 12
FACTOR = 1.0 / math.sqrt(512 * WORK_TILES)
GROUP = 8
STEPS = 3
PAD_TILES = GROUP * STEPS
ROWS = PAD_TILES * ACT_PIX
GROUP_ROWS = GROUP * ACT_PIX
DOT_ROWS = 192
COT_ROWS = PAD_TILES * OUT_PIX
GROUP_COT = GROUP * OUT_PIX
WINDOWS = ((0, 128), (80, 128), (160, 110))
PAIR_ROWS = 16 * TAPS
SHARE = 96
BF = jnp.bfloat16
F32 = jnp.float32


def selection():
    row = lax.broadcasted_iota(jnp.int32, (3, PAIR_ROWS, 128), 1)
    col = lax.broadcasted_iota(jnp.int32, (3, PAIR_ROWS, 128), 2)
    group = lax.broadcasted_iota(jnp.int32, (3, PAIR_ROWS, 128), 0)
    tap, cell = row // 16, row % 16
    frame, i, j = cell // 8, (cell // 4) % 2, cell % 4
    source = (2 * group + frame) * 45 + (2 * i + tap // 3) * 9 + 2 * j + tap % 3
    pick = (source == col + 80 * group).astype(BF)
    kind = lax.broadcasted_iota(jnp.int32, (3, 8, 128), 1)
    cell = lax.broadcasted_iota(jnp.int32, (3, 8, 128), 2) + 80 * lax.broadcasted_iota(
        jnp.int32, (3, 8, 128), 0
    )
    top = (kind == 0) & (cell % 45 < 9)
    left = (kind == 1) & (cell % 9 == 0)
    past = (kind == 2) & (cell < 90)
    return pick, (top | left | past).astype(F32)


def live_count(plan_ref):
    count = plan_ref[0, 0]
    for q in range(2):
        for w in range(16):
            count = jnp.maximum(count, plan_ref[q, w])
    return count + 1


def patch_kernel(flags_ref, plan_ref, tiles_hbm, cot_ref, pick_ref, mark_ref, perm_ref,
                 patch_hbm, patcht_hbm, cotl_ref, cotp_ref,
                 tiles_s, patch_ref, patcht_ref, sems, out_sems):
    copies = []
    for g in range(STEPS):
        first, last = g * GROUP, min((g + 1) * GROUP, OWNED)
        span = pl.ds(first, last - first)
        copies.append(pltpu.make_async_copy(tiles_hbm.at[span], tiles_s.at[span], sems.at[g]))
        copies[g].start()
    count = live_count(plan_ref)
    for slot in range(OWNED):
        cells = slice(slot * OUT_PIX, (slot + 1) * OUT_PIX)
        one = cot_ref[slot]
        cotl_ref[cells, :] = jnp.where(slot < count, one, jnp.zeros_like(one))
    cotl_ref[OWNED * OUT_PIX:, :] = jnp.zeros((OUT_PIX, C), BF)
    cotp_ref[...] = jnp.dot(cotl_ref[...], perm_ref[...], preferred_element_type=F32).astype(BF)
    writes = []
    for g in range(STEPS):
        copies[g].wait()
        for slot in range(g * GROUP, min((g + 1) * GROUP, OWNED)):
            off = [jnp.where(flags_ref[k, slot] > 0, 0.0, 1.0) for k in range(3)]
            for w, (first, size) in enumerate(WINDOWS):
                marks = mark_ref[w]
                out = marks[0:1] * off[0] + marks[1:2] * off[1] + marks[2:3] * off[2]
                keep = jnp.where(out > 0.0, 0.0, 1.0).astype(BF)
                chosen = (pick_ref[w] * keep)[:, :size]
                got = jnp.dot(chosen, tiles_s[slot, first:first + size, :],
                              preferred_element_type=F32).astype(BF)
                row = slot * ACT_PIX + 16 * w
                for tap in range(TAPS):
                    patch_ref[row:row + 16, tap * C:(tap + 1) * C] = got[tap * 16:(tap + 1) * 16]
        if g == STEPS - 1:
            patch_ref[OWNED * ACT_PIX:, :] = jnp.zeros((ACT_PIX, TAPS * C), BF)
        rows = slice(g * GROUP_ROWS, (g + 1) * GROUP_ROWS)
        for tap in range(TAPS):
            patcht_ref[tap * C:(tap + 1) * C, rows] = patch_ref[rows, tap * C:(tap + 1) * C].T
        span = pl.ds(g * GROUP_ROWS, GROUP_ROWS)
        writes.append(pltpu.make_async_copy(patch_ref.at[span, :], patch_hbm.at[span, :],
                                            out_sems.at[2 * g]))
        writes.append(pltpu.make_async_copy(patcht_ref.at[:, span], patcht_hbm.at[:, span],
                                            out_sems.at[2 * g + 1]))
        writes[2 * g].start()
        writes[2 * g + 1].start()
    for write in writes:
        write.wait()


def main_kernel(core_ref, plan_ref, got_ref, other_ref, cotl_ref, cotp_ref, perm_ref,
                patch_hbm, patcht_hbm, feat_ref, keep_ref, send_ref,
                patch_s, patcht_s, spatial_s, temporal_s, pair_s, gpre_s, sems):
    spans = [pl.ds(g * GROUP_ROWS, GROUP_ROWS) for g in range(STEPS)]
    copies = [pltpu.make_async_copy(patch_hbm.at[span, :], patch_s.at[span, :], sems.at[g])
              for g, span in enumerate(spans)]
    copies.append(pltpu.make_async_copy(patcht_hbm, patcht_s, sems.at[STEPS]))
    for copy in copies:
        copy.start()
    count = live_count(plan_ref)

    def place(low_ref, high_ref):
        for b in range(16):
            spatial_s[b * 144:b * 144 + SHARE, :] = low_ref[b]
            spatial_s[b * 144 + SHARE:(b + 1) * 144, :] = high_ref[b, 2 * SHARE - 176:SHARE - 32, :]
            temporal_s[b * 32:(b + 1) * 32, :] = high_ref[b, SHARE - 32:, :]

    @pl.when(core_ref[0] == 0)
    def _():
        place(got_ref, other_ref)

    @pl.when(core_ref[0] != 0)
    def _():
        place(other_ref, got_ref)

    for g in range(STEPS):
        copies[g].wait()
        rows = slice(g * GROUP_ROWS, (g + 1) * GROUP_ROWS)
        cells = slice(g * GROUP_COT, (g + 1) * GROUP_COT)
        pre = jnp.concatenate([
            jnp.dot(patch_s[r:r + DOT_ROWS, :], spatial_s[...], preferred_element_type=F32)
            for r in range(g * GROUP_ROWS, (g + 1) * GROUP_ROWS, DOT_ROWS)
        ], axis=0)
        sig = 1.0 / (1.0 + jnp.exp(-pre))
        act = (pre * sig).astype(BF)
        slope = sig * (1.0 + pre * (1.0 - sig))
        for t in range(GROUP):
            out = slice(g * GROUP_COT + t * OUT_PIX, g * GROUP_COT + (t + 1) * OUT_PIX)
            pair_s[out, :C] = act[t * ACT_PIX + 16:(t + 1) * ACT_PIX]
            pair_s[out, C:] = act[t * ACT_PIX:t * ACT_PIX + OUT_PIX]
        gpair = lax.dot_general(cotl_ref[cells, :], temporal_s[...], (((1,), (1,)), ((), ())),
                                preferred_element_type=F32)
        pieces = []
        for t in range(GROUP):
            a, b, c = t * OUT_PIX, t * OUT_PIX + 16, (t + 1) * OUT_PIX
            pieces.append(gpair[a:b, C:])
            pieces.append(gpair[a:b, :C] + gpair[b:c, C:])
            pieces.append(gpair[b:c, :C])
        gact = jnp.concatenate(pieces, axis=0)
        gpre = (gact * slope).astype(BF)
        gpre_s[rows, :] = jnp.dot(gpre, perm_ref[...], preferred_element_type=F32).astype(BF)
        feat = jnp.dot(pair_s[cells, :], temporal_s[...], preferred_element_type=F32).astype(BF)
        for t in range(GROUP):
            slot = g * GROUP + t
            if slot < OWNED:
                one = feat[t * OUT_PIX:(t + 1) * OUT_PIX]
                feat_ref[slot] = jnp.where(slot < count, one, jnp.zeros_like(one))

    def put(first, grad):
        last = first + grad.shape[0]
        for b in range(first // 144, (last - 1) // 144 + 1):
            lo, hi = max(first, 144 * b), min(last, 144 * (b + 1))
            piece = grad[lo - first:hi - first]
            keep_ref[b, lo - 144 * b:hi - 144 * b, :] = piece[:, :128]
            send_ref[b, lo - 144 * b:hi - 144 * b, :] = piece[:, 128:].astype(BF)

    temporal = lax.dot_general(pair_s[...], cotp_ref[...], (((0,), (0,)), ((), ())),
                               preferred_element_type=F32)
    for b in range(16):
        piece = temporal[b * 32:(b + 1) * 32]
        keep_ref[b, 144:, :] = piece[:, :128]
        send_ref[b, 144:, :] = piece[:, 128:].astype(BF)
    copies[STEPS].wait()
    for tap in range(TAPS):
        put(tap * C, jnp.dot(patcht_s[tap * C:(tap + 1) * C, :], gpre_s[...],
                             preferred_element_type=F32))


def make_patches(flags, plan, tiles, cotangent, pick, marks, perm):
    hbm = pl.BlockSpec(memory_space=pltpu.HBM)
    vmem = pl.BlockSpec(memory_space=pltpu.VMEM)
    smem = pl.BlockSpec(memory_space=pltpu.SMEM)
    return pl.pallas_call(
        patch_kernel,
        in_specs=[smem, smem, hbm, vmem, vmem, vmem, vmem],
        out_specs=[hbm, hbm, vmem, vmem],
        out_shape=[
            pltpu.HBM((ROWS, TAPS * C), BF),
            pltpu.HBM((TAPS * C, ROWS), BF),
            jax.ShapeDtypeStruct((COT_ROWS, C), BF),
            jax.ShapeDtypeStruct((COT_ROWS, C), BF),
        ],
        scratch_shapes=[
            pltpu.VMEM((OWNED, IN_PIX, C), BF),
            pltpu.VMEM((ROWS, TAPS * C), BF),
            pltpu.VMEM((TAPS * C, ROWS), BF),
            pltpu.SemaphoreType.DMA((STEPS,)),
            pltpu.SemaphoreType.DMA((2 * STEPS,)),
        ],
        compiler_params=pltpu.CompilerParams(vmem_limit_bytes=32 * 2**20),
        cost_estimate=pl.CostEstimate(flops=6 * 10**9, bytes_accessed=15 * 10**6, transcendentals=0),
        name="patches",
    )(flags, plan, pltpu.with_memory_space_constraint(tiles, pltpu.HBM), cotangent, pick, marks,
      perm)


def run_section(core, plan, got, other, cot_live, cot_perm, perm, patches, patches_t):
    hbm = pl.BlockSpec(memory_space=pltpu.HBM)
    vmem = pl.BlockSpec(memory_space=pltpu.VMEM)
    smem = pl.BlockSpec(memory_space=pltpu.SMEM)
    return pl.pallas_call(
        main_kernel,
        in_specs=[smem] * 2 + [vmem] * 5 + [hbm] * 2,
        out_specs=[vmem] * 3,
        out_shape=[
            jax.ShapeDtypeStruct((OWNED, OUT_PIX, C), BF),
            jax.ShapeDtypeStruct((16, 176, 128), F32),
            jax.ShapeDtypeStruct((16, 176, 128), BF),
        ],
        scratch_shapes=[
            pltpu.VMEM((ROWS, TAPS * C), BF),
            pltpu.VMEM((TAPS * C, ROWS), BF),
            pltpu.VMEM((TAPS * C, C), BF),
            pltpu.VMEM((2 * C, C), BF),
            pltpu.VMEM((COT_ROWS, 2 * C), BF),
            pltpu.VMEM((ROWS, C), BF),
            pltpu.SemaphoreType.DMA((STEPS + 1,)),
        ],
        compiler_params=pltpu.CompilerParams(vmem_limit_bytes=36 * 2**20),
        cost_estimate=pl.CostEstimate(flops=4 * 10**9, bytes_accessed=15 * 10**6, transcendentals=0),
        name="section",
    )(core, plan, got, other, cot_live, cot_perm, perm,
      pltpu.with_memory_space_constraint(patches, pltpu.HBM),
      pltpu.with_memory_space_constraint(patches_t, pltpu.HBM))


def spread_kernel(core_ref, spatial_hbm, temporal_hbm, out_hbm, rows_s, in_sems, out_sems):
    reads = [pltpu.make_async_copy(spatial_hbm, rows_s.at[pl.ds(0, 144)], in_sems.at[0]),
             pltpu.make_async_copy(temporal_hbm, rows_s.at[pl.ds(144, 32)], in_sems.at[1])]
    for copy in reads:
        copy.start()
    for copy in reads:
        copy.wait()

    def write(first):
        copies = [pltpu.make_async_copy(rows_s.at[pl.ds(first, SHARE)], out_hbm.at[b],
                                        out_sems.at[b])
                  for b in range(16)]
        for copy in copies:
            copy.start()
        for copy in copies:
            copy.wait()

    @pl.when(core_ref[0] == 0)
    def _():
        write(0)

    @pl.when(core_ref[0] != 0)
    def _():
        write(176 - SHARE)


def spread(core, spatial, temporal):
    smem = pl.BlockSpec(memory_space=pltpu.SMEM)
    hbm = pl.BlockSpec(memory_space=pltpu.HBM)
    return pl.pallas_call(
        spread_kernel,
        in_specs=[smem, hbm, hbm],
        out_specs=hbm,
        out_shape=pltpu.HBM((16, SHARE, C), BF),
        scratch_shapes=[
            pltpu.VMEM((176, C), BF),
            pltpu.SemaphoreType.DMA((2,)),
            pltpu.SemaphoreType.DMA((16,)),
        ],
        name="spread",
    )(core, pltpu.with_memory_space_constraint(spatial, pltpu.HBM),
      pltpu.with_memory_space_constraint(temporal, pltpu.HBM))


def permutation(core):
    row = lax.broadcasted_iota(jnp.int32, (C, C), 0)
    col = lax.broadcasted_iota(jnp.int32, (C, C), 1)
    wanted = ((col % 128) // 8) * 16 + jnp.bitwise_xor(core, col // 128) * 8 + col % 8
    return (row == wanted).astype(BF)


def per_device(tiles, cotangent, halo_flags, send_plan, spatial_weight, temporal_weight):
    core = lax.axis_index("dp") % 2
    siblings = [(i, i ^ 1) for i in range(32)]
    core_id = core.reshape(1).astype(jnp.int32)
    got = lax.all_to_all(spread(core_id, spatial_weight, temporal_weight), "bal", 0, 0)

    pick, marks = selection()
    perm = permutation(core)
    flags = halo_flags.T
    plan = send_plan[0].T
    patches, patches_t, cot_live, cot_perm = make_patches(
        flags, plan, tiles, cotangent, pick, marks, perm
    )
    got, cot_live = lax.optimization_barrier((got, cot_live))
    other = lax.ppermute(got, "dp", siblings)
    features, keep, send = run_section(
        core_id, plan, got, other, cot_live, cot_perm, perm,
        patches, patches_t
    )

    theirs = lax.ppermute(send, "dp", siblings)
    chip = (keep + theirs.astype(F32)).astype(BF)
    part = lax.all_to_all(chip, "bal", 0, 0)
    part = jnp.sum(part.astype(F32), axis=0)
    part = part.T.reshape(16, 8, 176)
    along_z = [[2 * z + c for z in range(16)] for c in range(2)]
    last = lax.all_to_all(part, "dp", 0, 0, axis_index_groups=along_z)
    total = jnp.sum(last, axis=0) * FACTOR
    return features, total[:, :144].T, total[:, 144:].T


def solution(mesh):
    in_specs = (
        P(("dp", "bal"), None, None),
        P(("dp", "bal"), None, None),
        P(("dp", "bal"), None),
        P(("dp", "bal"), None, None),
        P("bal", None),
        P("bal", None),
    )
    out_specs = (P(("dp", "bal"), None, None), P("bal", "dp"), P("bal", "dp"))
    return jax.shard_map(
        per_device, mesh=mesh, in_specs=in_specs, out_specs=out_specs, check_vma=False
    )
```

```python
import functools
import math

import jax
import jax.numpy as jnp
from jax import lax
from jax.experimental import pallas as pl
from jax.experimental.pallas import tpu as pltpu
from jax.sharding import PartitionSpec as P

C = 256
OWNED = 23
IN_PIX = 270
OUT_PIX = 32
ACT_PIX = 48
TAPS = 9
WORK_TILES = 12
FACTOR = 1.0 / math.sqrt(512 * WORK_TILES)
GROUP = 8
STEPS = 3
PAD_TILES = GROUP * STEPS
ROWS = PAD_TILES * ACT_PIX
GROUP_ROWS = GROUP * ACT_PIX
DOT_ROWS = 192
EARLY_ROWS = 2 * GROUP_ROWS
COT_ROWS = PAD_TILES * OUT_PIX
GROUP_COT = GROUP * OUT_PIX
WINDOWS = ((0, 128), (80, 128), (160, 110))
PAIR_ROWS = 16 * TAPS
SHARE = 96
BF = jnp.bfloat16
F32 = jnp.float32


def selection():
    row = lax.broadcasted_iota(jnp.int32, (3, PAIR_ROWS, 128), 1)
    col = lax.broadcasted_iota(jnp.int32, (3, PAIR_ROWS, 128), 2)
    group = lax.broadcasted_iota(jnp.int32, (3, PAIR_ROWS, 128), 0)
    tap, cell = row // 16, row % 16
    frame, i, j = cell // 8, (cell // 4) % 2, cell % 4
    source = (2 * group + frame) * 45 + (2 * i + tap // 3) * 9 + 2 * j + tap % 3
    pick = (source == col + 80 * group).astype(BF)
    kind = lax.broadcasted_iota(jnp.int32, (3, 8, 128), 1)
    cell = lax.broadcasted_iota(jnp.int32, (3, 8, 128), 2) + 80 * lax.broadcasted_iota(
        jnp.int32, (3, 8, 128), 0
    )
    top = (kind == 0) & (cell % 45 < 9)
    left = (kind == 1) & (cell % 9 == 0)
    past = (kind == 2) & (cell < 90)
    return pick, (top | left | past).astype(F32)


def live_count(plan_ref):
    count = plan_ref[0, 0]
    for q in range(2):
        for w in range(16):
            count = jnp.maximum(count, plan_ref[q, w])
    return count + 1


def patch_kernel(flags_ref, plan_ref, tiles_hbm, cot_ref, pick_ref, mark_ref, perm_ref,
                 patch_hbm, patcht_hbm, cotl_ref, cotp_ref,
                 tiles_s, patch_ref, patcht_ref, sems, out_sems):
    copies = []
    for g in range(STEPS):
        first, last = g * GROUP, min((g + 1) * GROUP, OWNED)
        span = pl.ds(first, last - first)
        copies.append(pltpu.make_async_copy(tiles_hbm.at[span], tiles_s.at[span], sems.at[g]))
        copies[g].start()
    count = live_count(plan_ref)
    for slot in range(OWNED):
        cells = slice(slot * OUT_PIX, (slot + 1) * OUT_PIX)
        one = cot_ref[slot]
        cotl_ref[cells, :] = jnp.where(slot < count, one, jnp.zeros_like(one))
    cotl_ref[OWNED * OUT_PIX:, :] = jnp.zeros((OUT_PIX, C), BF)
    cotp_ref[...] = jnp.dot(cotl_ref[...], perm_ref[...], preferred_element_type=F32).astype(BF)
    writes = []
    for g in range(STEPS):
        copies[g].wait()
        for slot in range(g * GROUP, min((g + 1) * GROUP, OWNED)):
            off = [jnp.where(flags_ref[k, slot] > 0, 0.0, 1.0) for k in range(3)]
            for w, (first, size) in enumerate(WINDOWS):
                marks = mark_ref[w]
                out = marks[0:1] * off[0] + marks[1:2] * off[1] + marks[2:3] * off[2]
                keep = jnp.where(out > 0.0, 0.0, 1.0).astype(BF)
                chosen = (pick_ref[w] * keep)[:, :size]
                got = jnp.dot(chosen, tiles_s[slot, first:first + size, :],
                              preferred_element_type=F32).astype(BF)
                row = slot * ACT_PIX + 16 * w
                for tap in range(TAPS):
                    patch_ref[row:row + 16, tap * C:(tap + 1) * C] = got[tap * 16:(tap + 1) * 16]
        if g == STEPS - 1:
            patch_ref[OWNED * ACT_PIX:, :] = jnp.zeros((ACT_PIX, TAPS * C), BF)
        rows = slice(g * GROUP_ROWS, (g + 1) * GROUP_ROWS)
        for tap in range(TAPS):
            patcht_ref[tap * C:(tap + 1) * C, rows] = patch_ref[rows, tap * C:(tap + 1) * C].T
        span = pl.ds(g * GROUP_ROWS, GROUP_ROWS)
        writes.append(pltpu.make_async_copy(patch_ref.at[span, :], patch_hbm.at[span, :],
                                            out_sems.at[2 * g]))
        writes.append(pltpu.make_async_copy(patcht_ref.at[:, span], patcht_hbm.at[:, span],
                                            out_sems.at[2 * g + 1]))
        writes[2 * g].start()
        writes[2 * g + 1].start()
    for write in writes:
        write.wait()


def fetch_kernel(patch_hbm, early_ref, sems):
    spans = [pl.ds(r, 96) for r in range(0, EARLY_ROWS, 96)]
    copies = [pltpu.make_async_copy(patch_hbm.at[span, :], early_ref.at[span, :], sems.at[k])
              for k, span in enumerate(spans)]
    for copy in copies:
        copy.start()
    for copy in copies:
        copy.wait()


def fetch(patches):
    return pl.pallas_call(
        fetch_kernel,
        in_specs=[pl.BlockSpec(memory_space=pltpu.HBM)],
        out_specs=pl.BlockSpec(memory_space=pltpu.VMEM),
        out_shape=jax.ShapeDtypeStruct((EARLY_ROWS, TAPS * C), BF),
        scratch_shapes=[pltpu.SemaphoreType.DMA((EARLY_ROWS // 96,))],
        compiler_params=pltpu.CompilerParams(vmem_limit_bytes=8 * 2**20),
        cost_estimate=pl.CostEstimate(flops=0, bytes_accessed=8 * 10**6, transcendentals=0),
        name="fetch",
    )(pltpu.with_memory_space_constraint(patches, pltpu.HBM))


def main_kernel(core_ref, plan_ref, got_ref, other_ref, cotl_ref, cotp_ref, perm_ref, early_ref,
                patch_hbm, patcht_hbm, feat_ref, keep_ref, send_ref,
                late_s, patcht_s, spatial_s, temporal_s, pair_s, gpre_s, sems):
    copies = [pltpu.make_async_copy(patch_hbm.at[pl.ds(EARLY_ROWS + r, 96), :],
                                    late_s.at[pl.ds(r, 96), :], sems.at[r // 96])
              for r in range(0, GROUP_ROWS, 96)]
    copies += [pltpu.make_async_copy(patcht_hbm.at[pl.ds(tap * C, C), :],
                                     patcht_s.at[pl.ds(tap * C, C), :], sems.at[4 + tap])
               for tap in range(TAPS)]
    for copy in copies:
        copy.start()
    count = live_count(plan_ref)

    def place(low_ref, high_ref):
        for b in range(16):
            spatial_s[b * 144:b * 144 + SHARE, :] = low_ref[b]
            spatial_s[b * 144 + SHARE:(b + 1) * 144, :] = high_ref[b, 2 * SHARE - 176:SHARE - 32, :]
            temporal_s[b * 32:(b + 1) * 32, :] = high_ref[b, SHARE - 32:, :]

    @pl.when(core_ref[0] == 0)
    def _():
        place(got_ref, other_ref)

    @pl.when(core_ref[0] != 0)
    def _():
        place(other_ref, got_ref)

    for g in range(STEPS):
        if g == STEPS - 1:
            for copy in copies:
                copy.wait()
        patch_ref = late_s if g == STEPS - 1 else early_ref
        base = 0 if g == STEPS - 1 else g * GROUP_ROWS
        rows = slice(g * GROUP_ROWS, (g + 1) * GROUP_ROWS)
        cells = slice(g * GROUP_COT, (g + 1) * GROUP_COT)
        pre = jnp.concatenate([
            jnp.dot(patch_ref[r:r + DOT_ROWS, :], spatial_s[...], preferred_element_type=F32)
            for r in range(base, base + GROUP_ROWS, DOT_ROWS)
        ], axis=0)
        sig = 1.0 / (1.0 + jnp.exp(-pre))
        act = (pre * sig).astype(BF)
        slope = sig * (1.0 + pre * (1.0 - sig))
        for t in range(GROUP):
            out = slice(g * GROUP_COT + t * OUT_PIX, g * GROUP_COT + (t + 1) * OUT_PIX)
            pair_s[out, :C] = act[t * ACT_PIX + 16:(t + 1) * ACT_PIX]
            pair_s[out, C:] = act[t * ACT_PIX:t * ACT_PIX + OUT_PIX]
        gpair = lax.dot_general(cotl_ref[cells, :], temporal_s[...], (((1,), (1,)), ((), ())),
                                preferred_element_type=F32)
        pieces = []
        for t in range(GROUP):
            a, b, c = t * OUT_PIX, t * OUT_PIX + 16, (t + 1) * OUT_PIX
            pieces.append(gpair[a:b, C:])
            pieces.append(gpair[a:b, :C] + gpair[b:c, C:])
            pieces.append(gpair[b:c, :C])
        gact = jnp.concatenate(pieces, axis=0)
        gpre = (gact * slope).astype(BF)
        gpre_s[rows, :] = jnp.dot(gpre, perm_ref[...], preferred_element_type=F32).astype(BF)
        feat = jnp.dot(pair_s[cells, :], temporal_s[...], preferred_element_type=F32).astype(BF)
        for t in range(GROUP):
            slot = g * GROUP + t
            if slot < OWNED:
                one = feat[t * OUT_PIX:(t + 1) * OUT_PIX]
                feat_ref[slot] = jnp.where(slot < count, one, jnp.zeros_like(one))

    def put(first, grad):
        last = first + grad.shape[0]
        for b in range(first // 144, (last - 1) // 144 + 1):
            lo, hi = max(first, 144 * b), min(last, 144 * (b + 1))
            piece = grad[lo - first:hi - first]
            keep_ref[b, lo - 144 * b:hi - 144 * b, :] = piece[:, :128]
            send_ref[b, lo - 144 * b:hi - 144 * b, :] = piece[:, 128:].astype(BF)

    temporal = lax.dot_general(pair_s[...], cotp_ref[...], (((0,), (0,)), ((), ())),
                               preferred_element_type=F32)
    for b in range(16):
        piece = temporal[b * 32:(b + 1) * 32]
        keep_ref[b, 144:, :] = piece[:, :128]
        send_ref[b, 144:, :] = piece[:, 128:].astype(BF)
    for tap in range(TAPS):
        put(tap * C, jnp.dot(patcht_s[tap * C:(tap + 1) * C, :], gpre_s[...],
                             preferred_element_type=F32))


def make_patches(flags, plan, tiles, cotangent, pick, marks, perm):
    hbm = pl.BlockSpec(memory_space=pltpu.HBM)
    vmem = pl.BlockSpec(memory_space=pltpu.VMEM)
    smem = pl.BlockSpec(memory_space=pltpu.SMEM)
    return pl.pallas_call(
        patch_kernel,
        in_specs=[smem, smem, hbm, vmem, vmem, vmem, vmem],
        out_specs=[hbm, hbm, vmem, vmem],
        out_shape=[
            pltpu.HBM((ROWS, TAPS * C), BF),
            pltpu.HBM((TAPS * C, ROWS), BF),
            jax.ShapeDtypeStruct((COT_ROWS, C), BF),
            jax.ShapeDtypeStruct((COT_ROWS, C), BF),
        ],
        scratch_shapes=[
            pltpu.VMEM((OWNED, IN_PIX, C), BF),
            pltpu.VMEM((ROWS, TAPS * C), BF),
            pltpu.VMEM((TAPS * C, ROWS), BF),
            pltpu.SemaphoreType.DMA((STEPS,)),
            pltpu.SemaphoreType.DMA((2 * STEPS,)),
        ],
        compiler_params=pltpu.CompilerParams(vmem_limit_bytes=32 * 2**20),
        cost_estimate=pl.CostEstimate(flops=6 * 10**9, bytes_accessed=15 * 10**6, transcendentals=0),
        name="patches",
    )(flags, plan, pltpu.with_memory_space_constraint(tiles, pltpu.HBM), cotangent, pick, marks,
      perm)


def run_section(core, plan, got, other, cot_live, cot_perm, perm, early, patches, patches_t):
    hbm = pl.BlockSpec(memory_space=pltpu.HBM)
    vmem = pl.BlockSpec(memory_space=pltpu.VMEM)
    smem = pl.BlockSpec(memory_space=pltpu.SMEM)
    return pl.pallas_call(
        main_kernel,
        in_specs=[smem] * 2 + [vmem] * 6 + [hbm] * 2,
        out_specs=[vmem] * 3,
        out_shape=[
            jax.ShapeDtypeStruct((OWNED, OUT_PIX, C), BF),
            jax.ShapeDtypeStruct((16, 176, 128), F32),
            jax.ShapeDtypeStruct((16, 176, 128), BF),
        ],
        scratch_shapes=[
            pltpu.VMEM((GROUP_ROWS, TAPS * C), BF),
            pltpu.VMEM((TAPS * C, ROWS), BF),
            pltpu.VMEM((TAPS * C, C), BF),
            pltpu.VMEM((2 * C, C), BF),
            pltpu.VMEM((COT_ROWS, 2 * C), BF),
            pltpu.VMEM((ROWS, C), BF),
            pltpu.SemaphoreType.DMA((4 + TAPS,)),
        ],
        compiler_params=pltpu.CompilerParams(vmem_limit_bytes=36 * 2**20),
        cost_estimate=pl.CostEstimate(flops=4 * 10**9, bytes_accessed=15 * 10**6, transcendentals=0),
        name="section",
    )(core, plan, got, other, cot_live, cot_perm, perm, early,
      pltpu.with_memory_space_constraint(patches, pltpu.HBM),
      pltpu.with_memory_space_constraint(patches_t, pltpu.HBM))


def spread_kernel(core_ref, spatial_hbm, temporal_hbm, out_ref, rows_s, sems):
    reads = [pltpu.make_async_copy(spatial_hbm, rows_s.at[pl.ds(0, 144)], sems.at[0]),
             pltpu.make_async_copy(temporal_hbm, rows_s.at[pl.ds(144, 32)], sems.at[1])]
    for copy in reads:
        copy.start()
    for copy in reads:
        copy.wait()

    def write(first):
        mine = rows_s[first:first + SHARE, :]
        for b in range(16):
            out_ref[b] = mine

    @pl.when(core_ref[0] == 0)
    def _():
        write(0)

    @pl.when(core_ref[0] != 0)
    def _():
        write(176 - SHARE)


def spread(core, spatial, temporal):
    smem = pl.BlockSpec(memory_space=pltpu.SMEM)
    hbm = pl.BlockSpec(memory_space=pltpu.HBM)
    return pl.pallas_call(
        spread_kernel,
        in_specs=[smem, hbm, hbm],
        out_specs=pl.BlockSpec(memory_space=pltpu.VMEM),
        out_shape=jax.ShapeDtypeStruct((16, SHARE, C), BF),
        scratch_shapes=[
            pltpu.VMEM((176, C), BF),
            pltpu.SemaphoreType.DMA((2,)),
        ],
        compiler_params=pltpu.CompilerParams(vmem_limit_bytes=8 * 2**20),
        name="spread",
    )(core, pltpu.with_memory_space_constraint(spatial, pltpu.HBM),
      pltpu.with_memory_space_constraint(temporal, pltpu.HBM))


def finish_kernel(part_ref, spatial_hbm, temporal_hbm, spatial_s, temporal_s, sems):
    total = part_ref[0]
    for z in range(1, part_ref.shape[0]):
        total = total + part_ref[z]
    total = total * FACTOR
    spatial_s[...] = total[:, :144]
    temporal_s[...] = total[:, 144:]
    copies = [pltpu.make_async_copy(spatial_s, spatial_hbm, sems.at[0]),
              pltpu.make_async_copy(temporal_s, temporal_hbm, sems.at[1])]
    for copy in copies:
        copy.start()
    for copy in copies:
        copy.wait()


def finish(part):
    hbm = pl.BlockSpec(memory_space=pltpu.HBM)
    return pl.pallas_call(
        finish_kernel,
        in_specs=[pl.BlockSpec(memory_space=pltpu.VMEM)],
        out_specs=[hbm, hbm],
        out_shape=[pltpu.HBM((8, 144), F32), pltpu.HBM((8, 32), F32)],
        scratch_shapes=[
            pltpu.VMEM((8, 144), F32),
            pltpu.VMEM((8, 32), F32),
            pltpu.SemaphoreType.DMA((2,)),
        ],
        compiler_params=pltpu.CompilerParams(vmem_limit_bytes=4 * 2**20),
        name="finish",
    )(part)


def permutation(core):
    row = lax.broadcasted_iota(jnp.int32, (C, C), 0)
    col = lax.broadcasted_iota(jnp.int32, (C, C), 1)
    wanted = ((col % 128) // 8) * 16 + jnp.bitwise_xor(core, col // 128) * 8 + col % 8
    return (row == wanted).astype(BF)


def per_device(tiles, cotangent, halo_flags, send_plan, spatial_weight, temporal_weight):
    core = lax.axis_index("dp") % 2
    siblings = [(i, i ^ 1) for i in range(32)]
    core_id = core.reshape(1).astype(jnp.int32)
    got = lax.all_to_all(spread(core_id, spatial_weight, temporal_weight), "bal", 0, 0)

    pick, marks = selection()
    perm = permutation(core)
    flags = halo_flags.T
    plan = send_plan[0].T
    patches, patches_t, cot_live, cot_perm = make_patches(
        flags, plan, tiles, cotangent, pick, marks, perm
    )
    got, patches, patches_t = lax.optimization_barrier((got, patches, patches_t))
    other = lax.ppermute(got, "dp", siblings)
    features, keep, send = run_section(
        core_id, plan, got, other, cot_live, cot_perm, perm, fetch(patches), patches, patches_t
    )

    theirs = lax.ppermute(send, "dp", siblings)
    chip = (keep + theirs.astype(F32)).astype(BF)
    part = lax.all_to_all(chip, "bal", 0, 0)
    part = jnp.sum(part.astype(F32), axis=0)
    part = part.T.reshape(16, 8, 176)
    along_z = [[2 * z + c for z in range(16)] for c in range(2)]
    last = lax.all_to_all(part, "dp", 0, 0, axis_index_groups=along_z)
    spatial_t, temporal_t = finish(last)
    return features, spatial_t.T, temporal_t.T


def solution(mesh):
    in_specs = (
        P(("dp", "bal"), None, None),
        P(("dp", "bal"), None, None),
        P(("dp", "bal"), None),
        P(("dp", "bal"), None, None),
        P("bal", None),
        P("bal", None),
    )
    out_specs = (P(("dp", "bal"), None, None), P("bal", "dp"), P("bal", "dp"))
    return jax.shard_map(
        per_device, mesh=mesh, in_specs=in_specs, out_specs=out_specs, check_vma=False
    )
```

```python
import functools
import math

import jax
import jax.numpy as jnp
from jax import lax
from jax.experimental import pallas as pl
from jax.experimental.pallas import tpu as pltpu
from jax.sharding import PartitionSpec as P

C = 256
OWNED = 23
IN_PIX = 270
OUT_PIX = 32
ACT_PIX = 48
TAPS = 9
WORK_TILES = 12
FACTOR = 1.0 / math.sqrt(512 * WORK_TILES)
GROUP = 8
STEPS = 3
PAD_TILES = GROUP * STEPS
ROWS = PAD_TILES * ACT_PIX
GROUP_ROWS = GROUP * ACT_PIX
DOT_ROWS = 192
REST_ROWS = ROWS - GROUP_ROWS
COT_ROWS = PAD_TILES * OUT_PIX
GROUP_COT = GROUP * OUT_PIX
WINDOWS = ((0, 128), (80, 128), (160, 110))
PAIR_ROWS = 16 * TAPS
SHARE = 96
BF = jnp.bfloat16
F32 = jnp.float32


def selection():
    row = lax.broadcasted_iota(jnp.int32, (3, PAIR_ROWS, 128), 1)
    col = lax.broadcasted_iota(jnp.int32, (3, PAIR_ROWS, 128), 2)
    group = lax.broadcasted_iota(jnp.int32, (3, PAIR_ROWS, 128), 0)
    tap, cell = row // 16, row % 16
    frame, i, j = cell // 8, (cell // 4) % 2, cell % 4
    source = (2 * group + frame) * 45 + (2 * i + tap // 3) * 9 + 2 * j + tap % 3
    pick = (source == col + 80 * group).astype(BF)
    kind = lax.broadcasted_iota(jnp.int32, (3, 8, 128), 1)
    cell = lax.broadcasted_iota(jnp.int32, (3, 8, 128), 2) + 80 * lax.broadcasted_iota(
        jnp.int32, (3, 8, 128), 0
    )
    top = (kind == 0) & (cell % 45 < 9)
    left = (kind == 1) & (cell % 9 == 0)
    past = (kind == 2) & (cell < 90)
    return pick, (top | left | past).astype(F32)


def live_count(plan_ref):
    count = plan_ref[0, 0]
    for q in range(2):
        for w in range(16):
            count = jnp.maximum(count, plan_ref[q, w])
    return count + 1


def patch_kernel(flags_ref, plan_ref, tiles_hbm, cot_ref, pick_ref, mark_ref,
                 first_ref, patch_hbm, patcht_hbm, cotl_ref,
                 tiles_s, patch_s, patcht_ref, sems, out_sems):
    copies = []
    for g in range(STEPS):
        first, last = g * GROUP, min((g + 1) * GROUP, OWNED)
        span = pl.ds(first, last - first)
        copies.append(pltpu.make_async_copy(tiles_hbm.at[span], tiles_s.at[span], sems.at[g]))
        copies[g].start()
    count = live_count(plan_ref)
    for slot in range(OWNED):
        cells = slice(slot * OUT_PIX, (slot + 1) * OUT_PIX)
        one = cot_ref[slot]
        cotl_ref[cells, :] = jnp.where(slot < count, one, jnp.zeros_like(one))
    cotl_ref[OWNED * OUT_PIX:, :] = jnp.zeros((OUT_PIX, C), BF)
    writes = []
    for g in range(STEPS):
        copies[g].wait()
        patch_ref = first_ref if g == 0 else patch_s
        base = 0 if g == 0 else (g - 1) * GROUP_ROWS
        for slot in range(g * GROUP, min((g + 1) * GROUP, OWNED)):
            off = [jnp.where(flags_ref[k, slot] > 0, 0.0, 1.0) for k in range(3)]
            for w, (first, size) in enumerate(WINDOWS):
                marks = mark_ref[w]
                out = marks[0:1] * off[0] + marks[1:2] * off[1] + marks[2:3] * off[2]
                keep = jnp.where(out > 0.0, 0.0, 1.0).astype(BF)
                chosen = (pick_ref[w] * keep)[:, :size]
                got = jnp.dot(chosen, tiles_s[slot, first:first + size, :],
                              preferred_element_type=F32).astype(BF)
                row = base + (slot - g * GROUP) * ACT_PIX + 16 * w
                for tap in range(TAPS):
                    patch_ref[row:row + 16, tap * C:(tap + 1) * C] = got[tap * 16:(tap + 1) * 16]
        if g == STEPS - 1:
            patch_ref[REST_ROWS - ACT_PIX:, :] = jnp.zeros((ACT_PIX, TAPS * C), BF)
        rows = slice(g * GROUP_ROWS, (g + 1) * GROUP_ROWS)
        for tap in range(TAPS):
            patcht_ref[tap * C:(tap + 1) * C, rows] = \
                patch_ref[base:base + GROUP_ROWS, tap * C:(tap + 1) * C].T
        span = pl.ds(g * GROUP_ROWS, GROUP_ROWS)
        started = [pltpu.make_async_copy(patcht_ref.at[:, span], patcht_hbm.at[:, span],
                                         out_sems.at[2 * g])]
        if g:
            span = pl.ds(base, GROUP_ROWS)
            started.append(pltpu.make_async_copy(patch_s.at[span, :], patch_hbm.at[span, :],
                                                 out_sems.at[2 * g + 1]))
        for write in started:
            write.start()
        writes += started
    for write in writes:
        write.wait()


def fetch_kernel(patch_hbm, rest_ref, sems):
    spans = [pl.ds(r, 96) for r in range(0, REST_ROWS, 96)]
    copies = [pltpu.make_async_copy(patch_hbm.at[span, :], rest_ref.at[span, :], sems.at[k])
              for k, span in enumerate(spans)]
    for copy in copies:
        copy.start()
    for copy in copies:
        copy.wait()


def fetch(patches):
    return pl.pallas_call(
        fetch_kernel,
        in_specs=[pl.BlockSpec(memory_space=pltpu.HBM)],
        out_specs=pl.BlockSpec(memory_space=pltpu.VMEM),
        out_shape=jax.ShapeDtypeStruct((REST_ROWS, TAPS * C), BF),
        scratch_shapes=[pltpu.SemaphoreType.DMA((REST_ROWS // 96,))],
        compiler_params=pltpu.CompilerParams(vmem_limit_bytes=8 * 2**20),
        cost_estimate=pl.CostEstimate(flops=0, bytes_accessed=8 * 10**6, transcendentals=0),
        name="fetch",
    )(pltpu.with_memory_space_constraint(patches, pltpu.HBM))


def main_kernel(core_ref, plan_ref, got_ref, other_ref, cotl_ref, perm_ref, first_ref, rest_ref,
                patcht_hbm, feat_ref, keep_ref, send_ref,
                patcht_s, spatial_s, temporal_s, pair_s, gpre_s, cotp_s, sems):
    copies = [pltpu.make_async_copy(patcht_hbm.at[pl.ds(tap * C, C), :],
                                    patcht_s.at[pl.ds(tap * C, C), :], sems.at[tap])
              for tap in range(TAPS)]
    for copy in copies:
        copy.start()
    count = live_count(plan_ref)

    def place(low_ref, high_ref):
        for b in range(16):
            spatial_s[b * 144:b * 144 + SHARE, :] = low_ref[b]
            spatial_s[b * 144 + SHARE:(b + 1) * 144, :] = high_ref[b, 2 * SHARE - 176:SHARE - 32, :]
            temporal_s[b * 32:(b + 1) * 32, :] = high_ref[b, SHARE - 32:, :]

    @pl.when(core_ref[0] == 0)
    def _():
        place(got_ref, other_ref)

    @pl.when(core_ref[0] != 0)
    def _():
        place(other_ref, got_ref)

    for g in range(STEPS):
        patch_ref = rest_ref if g else first_ref
        base = (g - 1) * GROUP_ROWS if g else 0
        rows = slice(g * GROUP_ROWS, (g + 1) * GROUP_ROWS)
        cells = slice(g * GROUP_COT, (g + 1) * GROUP_COT)
        pre = jnp.concatenate([
            jnp.dot(patch_ref[r:r + DOT_ROWS, :], spatial_s[...], preferred_element_type=F32)
            for r in range(base, base + GROUP_ROWS, DOT_ROWS)
        ], axis=0)
        sig = 1.0 / (1.0 + jnp.exp(-pre))
        act = (pre * sig).astype(BF)
        slope = sig * (1.0 + pre * (1.0 - sig))
        for t in range(GROUP):
            out = slice(g * GROUP_COT + t * OUT_PIX, g * GROUP_COT + (t + 1) * OUT_PIX)
            pair_s[out, :C] = act[t * ACT_PIX + 16:(t + 1) * ACT_PIX]
            pair_s[out, C:] = act[t * ACT_PIX:t * ACT_PIX + OUT_PIX]
        gpair = lax.dot_general(cotl_ref[cells, :], temporal_s[...], (((1,), (1,)), ((), ())),
                                preferred_element_type=F32)
        pieces = []
        for t in range(GROUP):
            a, b, c = t * OUT_PIX, t * OUT_PIX + 16, (t + 1) * OUT_PIX
            pieces.append(gpair[a:b, C:])
            pieces.append(gpair[a:b, :C] + gpair[b:c, C:])
            pieces.append(gpair[b:c, :C])
        gact = jnp.concatenate(pieces, axis=0)
        gpre = (gact * slope).astype(BF)
        gpre_s[rows, :] = jnp.dot(gpre, perm_ref[...], preferred_element_type=F32).astype(BF)
        feat = jnp.dot(pair_s[cells, :], temporal_s[...], preferred_element_type=F32).astype(BF)
        for t in range(GROUP):
            slot = g * GROUP + t
            if slot < OWNED:
                one = feat[t * OUT_PIX:(t + 1) * OUT_PIX]
                feat_ref[slot] = jnp.where(slot < count, one, jnp.zeros_like(one))

    def put(first, grad):
        last = first + grad.shape[0]
        for b in range(first // 144, (last - 1) // 144 + 1):
            lo, hi = max(first, 144 * b), min(last, 144 * (b + 1))
            piece = grad[lo - first:hi - first]
            keep_ref[b, lo - 144 * b:hi - 144 * b, :] = piece[:, :128]
            send_ref[b, lo - 144 * b:hi - 144 * b, :] = piece[:, 128:].astype(BF)

    cotp_s[...] = jnp.dot(cotl_ref[...], perm_ref[...], preferred_element_type=F32).astype(BF)
    temporal = lax.dot_general(pair_s[...], cotp_s[...], (((0,), (0,)), ((), ())),
                               preferred_element_type=F32)
    for b in range(16):
        piece = temporal[b * 32:(b + 1) * 32]
        keep_ref[b, 144:, :] = piece[:, :128]
        send_ref[b, 144:, :] = piece[:, 128:].astype(BF)
    for copy in copies:
        copy.wait()
    for tap in range(TAPS):
        put(tap * C, jnp.dot(patcht_s[tap * C:(tap + 1) * C, :], gpre_s[...],
                             preferred_element_type=F32))


def make_patches(flags, plan, tiles, cotangent, pick, marks):
    hbm = pl.BlockSpec(memory_space=pltpu.HBM)
    vmem = pl.BlockSpec(memory_space=pltpu.VMEM)
    smem = pl.BlockSpec(memory_space=pltpu.SMEM)
    return pl.pallas_call(
        patch_kernel,
        in_specs=[smem, smem, hbm, vmem, vmem, vmem],
        out_specs=[vmem, hbm, hbm, vmem],
        out_shape=[
            jax.ShapeDtypeStruct((GROUP_ROWS, TAPS * C), BF),
            pltpu.HBM((REST_ROWS, TAPS * C), BF),
            pltpu.HBM((TAPS * C, ROWS), BF),
            jax.ShapeDtypeStruct((COT_ROWS, C), BF),
        ],
        scratch_shapes=[
            pltpu.VMEM((OWNED, IN_PIX, C), BF),
            pltpu.VMEM((REST_ROWS, TAPS * C), BF),
            pltpu.VMEM((TAPS * C, ROWS), BF),
            pltpu.SemaphoreType.DMA((STEPS,)),
            pltpu.SemaphoreType.DMA((2 * STEPS,)),
        ],
        compiler_params=pltpu.CompilerParams(vmem_limit_bytes=32 * 2**20),
        cost_estimate=pl.CostEstimate(flops=6 * 10**9, bytes_accessed=15 * 10**6, transcendentals=0),
        name="patches",
    )(flags, plan, pltpu.with_memory_space_constraint(tiles, pltpu.HBM), cotangent, pick, marks)


def run_section(core, plan, got, other, cot_live, perm, first, rest, patches_t):
    hbm = pl.BlockSpec(memory_space=pltpu.HBM)
    vmem = pl.BlockSpec(memory_space=pltpu.VMEM)
    smem = pl.BlockSpec(memory_space=pltpu.SMEM)
    return pl.pallas_call(
        main_kernel,
        in_specs=[smem] * 2 + [vmem] * 6 + [hbm],
        out_specs=[vmem] * 3,
        out_shape=[
            jax.ShapeDtypeStruct((OWNED, OUT_PIX, C), BF),
            jax.ShapeDtypeStruct((16, 176, 128), F32),
            jax.ShapeDtypeStruct((16, 176, 128), BF),
        ],
        scratch_shapes=[
            pltpu.VMEM((TAPS * C, ROWS), BF),
            pltpu.VMEM((TAPS * C, C), BF),
            pltpu.VMEM((2 * C, C), BF),
            pltpu.VMEM((COT_ROWS, 2 * C), BF),
            pltpu.VMEM((ROWS, C), BF),
            pltpu.VMEM((COT_ROWS, C), BF),
            pltpu.SemaphoreType.DMA((TAPS,)),
        ],
        compiler_params=pltpu.CompilerParams(vmem_limit_bytes=36 * 2**20),
        cost_estimate=pl.CostEstimate(flops=4 * 10**9, bytes_accessed=15 * 10**6, transcendentals=0),
        name="section",
    )(core, plan, got, other, cot_live, perm, first, rest,
      pltpu.with_memory_space_constraint(patches_t, pltpu.HBM))


def spread_kernel(core_ref, spatial_hbm, temporal_hbm, out_ref, rows_s, sems):
    reads = [pltpu.make_async_copy(spatial_hbm, rows_s.at[pl.ds(0, 144)], sems.at[0]),
             pltpu.make_async_copy(temporal_hbm, rows_s.at[pl.ds(144, 32)], sems.at[1])]
    for copy in reads:
        copy.start()
    for copy in reads:
        copy.wait()

    def write(first):
        mine = rows_s[first:first + SHARE, :]
        for b in range(16):
            out_ref[b] = mine

    @pl.when(core_ref[0] == 0)
    def _():
        write(0)

    @pl.when(core_ref[0] != 0)
    def _():
        write(176 - SHARE)


def spread(core, spatial, temporal):
    smem = pl.BlockSpec(memory_space=pltpu.SMEM)
    hbm = pl.BlockSpec(memory_space=pltpu.HBM)
    return pl.pallas_call(
        spread_kernel,
        in_specs=[smem, hbm, hbm],
        out_specs=pl.BlockSpec(memory_space=pltpu.VMEM),
        out_shape=jax.ShapeDtypeStruct((16, SHARE, C), BF),
        scratch_shapes=[
            pltpu.VMEM((176, C), BF),
            pltpu.SemaphoreType.DMA((2,)),
        ],
        compiler_params=pltpu.CompilerParams(vmem_limit_bytes=8 * 2**20),
        name="spread",
    )(core, pltpu.with_memory_space_constraint(spatial, pltpu.HBM),
      pltpu.with_memory_space_constraint(temporal, pltpu.HBM))


def finish_kernel(part_ref, spatial_hbm, temporal_hbm, spatial_s, temporal_s, sems):
    total = part_ref[0]
    for z in range(1, part_ref.shape[0]):
        total = total + part_ref[z]
    total = total * FACTOR
    spatial_s[...] = total[:, :144]
    temporal_s[...] = total[:, 144:]
    copies = [pltpu.make_async_copy(spatial_s, spatial_hbm, sems.at[0]),
              pltpu.make_async_copy(temporal_s, temporal_hbm, sems.at[1])]
    for copy in copies:
        copy.start()
    for copy in copies:
        copy.wait()


def finish(part):
    hbm = pl.BlockSpec(memory_space=pltpu.HBM)
    return pl.pallas_call(
        finish_kernel,
        in_specs=[pl.BlockSpec(memory_space=pltpu.VMEM)],
        out_specs=[hbm, hbm],
        out_shape=[pltpu.HBM((8, 144), F32), pltpu.HBM((8, 32), F32)],
        scratch_shapes=[
            pltpu.VMEM((8, 144), F32),
            pltpu.VMEM((8, 32), F32),
            pltpu.SemaphoreType.DMA((2,)),
        ],
        compiler_params=pltpu.CompilerParams(vmem_limit_bytes=4 * 2**20),
        name="finish",
    )(part)


def permutation(core):
    row = lax.broadcasted_iota(jnp.int32, (C, C), 0)
    col = lax.broadcasted_iota(jnp.int32, (C, C), 1)
    wanted = ((col % 128) // 8) * 16 + jnp.bitwise_xor(core, col // 128) * 8 + col % 8
    return (row == wanted).astype(BF)


def per_device(tiles, cotangent, halo_flags, send_plan, spatial_weight, temporal_weight):
    core = lax.axis_index("dp") % 2
    siblings = [(i, i ^ 1) for i in range(32)]
    core_id = core.reshape(1).astype(jnp.int32)
    got = lax.all_to_all(spread(core_id, spatial_weight, temporal_weight), "bal", 0, 0)

    pick, marks = selection()
    perm = permutation(core)
    flags = halo_flags.T
    plan = send_plan[0].T
    first, patches, patches_t, cot_live = make_patches(
        flags, plan, tiles, cotangent, pick, marks
    )
    got, patches, patches_t = lax.optimization_barrier((got, patches, patches_t))
    other = lax.ppermute(got, "dp", siblings)
    features, keep, send = run_section(
        core_id, plan, got, other, cot_live, perm, first, fetch(patches), patches_t
    )

    theirs = lax.ppermute(send, "dp", siblings)
    chip = (keep + theirs.astype(F32)).astype(BF)
    part = lax.all_to_all(chip, "bal", 0, 0)
    part = jnp.sum(part.astype(F32), axis=0)
    part = part.T.reshape(16, 8, 176)
    along_z = [[2 * z + c for z in range(16)] for c in range(2)]
    last = lax.all_to_all(part, "dp", 0, 0, axis_index_groups=along_z)
    spatial_t, temporal_t = finish(last)
    return features, spatial_t.T, temporal_t.T


def solution(mesh):
    in_specs = (
        P(("dp", "bal"), None, None),
        P(("dp", "bal"), None, None),
        P(("dp", "bal"), None),
        P(("dp", "bal"), None, None),
        P("bal", None),
        P("bal", None),
    )
    out_specs = (P(("dp", "bal"), None, None), P("bal", "dp"), P("bal", "dp"))
    return jax.shard_map(
        per_device, mesh=mesh, in_specs=in_specs, out_specs=out_specs, check_vma=False
    )
```

```python
import functools
import math

import jax
import jax.numpy as jnp
from jax import lax
from jax.experimental import pallas as pl
from jax.experimental.pallas import tpu as pltpu
from jax.sharding import PartitionSpec as P

C = 256
OWNED = 23
IN_PIX = 270
OUT_PIX = 32
ACT_PIX = 48
TAPS = 9
WORK_TILES = 12
FACTOR = 1.0 / math.sqrt(512 * WORK_TILES)
GROUP = 8
STEPS = 3
PAD_TILES = GROUP * STEPS
ROWS = PAD_TILES * ACT_PIX
GROUP_ROWS = GROUP * ACT_PIX
DOT_ROWS = 192
REST_ROWS = ROWS - GROUP_ROWS
COT_ROWS = PAD_TILES * OUT_PIX
GROUP_COT = GROUP * OUT_PIX
WINDOWS = ((0, 128), (80, 128), (160, 110))
PAIR_ROWS = 16 * TAPS
SHARE = 96
BF = jnp.bfloat16
F32 = jnp.float32


def selection():
    row = lax.broadcasted_iota(jnp.int32, (3, PAIR_ROWS, 128), 1)
    col = lax.broadcasted_iota(jnp.int32, (3, PAIR_ROWS, 128), 2)
    group = lax.broadcasted_iota(jnp.int32, (3, PAIR_ROWS, 128), 0)
    tap, cell = row // 16, row % 16
    frame, i, j = cell // 8, (cell // 4) % 2, cell % 4
    source = (2 * group + frame) * 45 + (2 * i + tap // 3) * 9 + 2 * j + tap % 3
    pick = (source == col + 80 * group).astype(BF)
    kind = lax.broadcasted_iota(jnp.int32, (3, 8, 128), 1)
    cell = lax.broadcasted_iota(jnp.int32, (3, 8, 128), 2) + 80 * lax.broadcasted_iota(
        jnp.int32, (3, 8, 128), 0
    )
    top = (kind == 0) & (cell % 45 < 9)
    left = (kind == 1) & (cell % 9 == 0)
    past = (kind == 2) & (cell < 90)
    return pick, (top | left | past).astype(F32)


def live_count(plan_ref):
    count = plan_ref[0, 0]
    for q in range(2):
        for w in range(16):
            count = jnp.maximum(count, plan_ref[q, w])
    return count + 1


def patch_kernel(flags_ref, plan_ref, tiles_hbm, cot_ref, pick_ref, mark_ref,
                 first_ref, patch_hbm, patcht_hbm, cotl_ref,
                 tiles_s, patch_s, patcht_ref, sems, out_sems):
    copies = []
    for g in range(STEPS):
        first, last = g * GROUP, min((g + 1) * GROUP, OWNED)
        span = pl.ds(first, last - first)
        copies.append(pltpu.make_async_copy(tiles_hbm.at[span], tiles_s.at[span], sems.at[g]))
        copies[g].start()
    count = live_count(plan_ref)
    for slot in range(OWNED):
        cells = slice(slot * OUT_PIX, (slot + 1) * OUT_PIX)
        one = cot_ref[slot]
        cotl_ref[cells, :] = jnp.where(slot < count, one, jnp.zeros_like(one))
    cotl_ref[OWNED * OUT_PIX:, :] = jnp.zeros((OUT_PIX, C), BF)
    writes = []
    for g in range(STEPS):
        copies[g].wait()
        patch_ref = first_ref if g == 0 else patch_s
        base = 0 if g == 0 else (g - 1) * GROUP_ROWS
        for slot in range(g * GROUP, min((g + 1) * GROUP, OWNED)):
            off = [jnp.where(flags_ref[k, slot] > 0, 0.0, 1.0) for k in range(3)]
            for w, (first, size) in enumerate(WINDOWS):
                marks = mark_ref[w]
                out = marks[0:1] * off[0] + marks[1:2] * off[1] + marks[2:3] * off[2]
                keep = jnp.where(out > 0.0, 0.0, 1.0).astype(BF)
                chosen = (pick_ref[w] * keep)[:, :size]
                got = jnp.dot(chosen, tiles_s[slot, first:first + size, :],
                              preferred_element_type=F32).astype(BF)
                row = base + (slot - g * GROUP) * ACT_PIX + 16 * w
                for tap in range(TAPS):
                    patch_ref[row:row + 16, tap * C:(tap + 1) * C] = got[tap * 16:(tap + 1) * 16]
        if g == STEPS - 1:
            patch_ref[REST_ROWS - ACT_PIX:, :] = jnp.zeros((ACT_PIX, TAPS * C), BF)
        rows = slice(g * GROUP_ROWS, (g + 1) * GROUP_ROWS)
        for tap in range(TAPS):
            patcht_ref[tap * C:(tap + 1) * C, rows] = \
                patch_ref[base:base + GROUP_ROWS, tap * C:(tap + 1) * C].T
        span = pl.ds(g * GROUP_ROWS, GROUP_ROWS)
        started = [pltpu.make_async_copy(patcht_ref.at[:, span], patcht_hbm.at[:, span],
                                         out_sems.at[2 * g])]
        if g:
            span = pl.ds(base, GROUP_ROWS)
            started.append(pltpu.make_async_copy(patch_s.at[span, :], patch_hbm.at[span, :],
                                                 out_sems.at[2 * g + 1]))
        for write in started:
            write.start()
        writes += started
    for write in writes:
        write.wait()


def fetch_kernel(first_ref, patch_hbm, all_ref, sems):
    copies = [pltpu.make_async_copy(patch_hbm.at[pl.ds(r, 96), :],
                                    all_ref.at[pl.ds(GROUP_ROWS + r, 96), :], sems.at[r // 96])
              for r in range(0, REST_ROWS, 96)]
    copies += [pltpu.make_async_copy(first_ref.at[pl.ds(r, 96), :], all_ref.at[pl.ds(r, 96), :],
                                     sems.at[(REST_ROWS + r) // 96])
               for r in range(0, GROUP_ROWS, 96)]
    for copy in copies:
        copy.start()
    for copy in copies:
        copy.wait()


def fetch(first, patches):
    return pl.pallas_call(
        fetch_kernel,
        in_specs=[pl.BlockSpec(memory_space=pltpu.VMEM), pl.BlockSpec(memory_space=pltpu.HBM)],
        out_specs=pl.BlockSpec(memory_space=pltpu.VMEM),
        out_shape=jax.ShapeDtypeStruct((ROWS, TAPS * C), BF),
        scratch_shapes=[pltpu.SemaphoreType.DMA((ROWS // 96,))],
        compiler_params=pltpu.CompilerParams(vmem_limit_bytes=8 * 2**20),
        cost_estimate=pl.CostEstimate(flops=0, bytes_accessed=8 * 10**6, transcendentals=0),
        name="fetch",
    )(first, pltpu.with_memory_space_constraint(patches, pltpu.HBM))


def main_kernel(core_ref, plan_ref, got_ref, other_ref, cotl_ref, perm_ref, patch_ref,
                patcht_hbm, feat_hbm, keep_ref, send_ref,
                feat_s, patcht_s, spatial_s, temporal_s, pair_s, gpre_s, cotp_s, sems):
    copies = [pltpu.make_async_copy(patcht_hbm.at[pl.ds(tap * C, C), :],
                                    patcht_s.at[pl.ds(tap * C, C), :], sems.at[tap])
              for tap in range(TAPS)]
    for copy in copies:
        copy.start()
    count = live_count(plan_ref)

    def place(low_ref, high_ref):
        for b in range(16):
            spatial_s[b * 144:b * 144 + SHARE, :] = low_ref[b]
            spatial_s[b * 144 + SHARE:(b + 1) * 144, :] = high_ref[b, 2 * SHARE - 176:SHARE - 32, :]
            temporal_s[b * 32:(b + 1) * 32, :] = high_ref[b, SHARE - 32:, :]

    @pl.when(core_ref[0] == 0)
    def _():
        place(got_ref, other_ref)

    @pl.when(core_ref[0] != 0)
    def _():
        place(other_ref, got_ref)

    pre = jnp.concatenate([
        jnp.dot(patch_ref[r:r + DOT_ROWS, :], spatial_s[...], preferred_element_type=F32)
        for r in range(0, ROWS, DOT_ROWS)
    ], axis=0)
    sig = 1.0 / (1.0 + jnp.exp(-pre))
    act = (pre * sig).astype(BF)
    slope = sig * (1.0 + pre * (1.0 - sig))
    gpair = lax.dot_general(cotl_ref[...], temporal_s[...], (((1,), (1,)), ((), ())),
                            preferred_element_type=F32)
    pieces = []
    for t in range(PAD_TILES):
        cells = slice(t * OUT_PIX, (t + 1) * OUT_PIX)
        pair_s[cells, :C] = act[t * ACT_PIX + 16:(t + 1) * ACT_PIX]
        pair_s[cells, C:] = act[t * ACT_PIX:t * ACT_PIX + OUT_PIX]
        a, b, c = t * OUT_PIX, t * OUT_PIX + 16, (t + 1) * OUT_PIX
        pieces.append(gpair[a:b, C:])
        pieces.append(gpair[a:b, :C] + gpair[b:c, C:])
        pieces.append(gpair[b:c, :C])
    gpre = (jnp.concatenate(pieces, axis=0) * slope).astype(BF)
    gpre_s[...] = jnp.dot(gpre, perm_ref[...], preferred_element_type=F32).astype(BF)
    feat = jnp.dot(pair_s[...], temporal_s[...], preferred_element_type=F32).astype(BF)
    for slot in range(OWNED):
        one = feat[slot * OUT_PIX:(slot + 1) * OUT_PIX]
        feat_s[slot] = jnp.where(slot < count, one, jnp.zeros_like(one))
    output = pltpu.make_async_copy(feat_s, feat_hbm, sems.at[TAPS])
    output.start()

    def put(first, grad):
        last = first + grad.shape[0]
        for b in range(first // 144, (last - 1) // 144 + 1):
            lo, hi = max(first, 144 * b), min(last, 144 * (b + 1))
            piece = grad[lo - first:hi - first]
            keep_ref[b, lo - 144 * b:hi - 144 * b, :] = piece[:, :128]
            send_ref[b, lo - 144 * b:hi - 144 * b, :] = piece[:, 128:].astype(BF)

    cotp_s[...] = jnp.dot(cotl_ref[...], perm_ref[...], preferred_element_type=F32).astype(BF)
    temporal = lax.dot_general(pair_s[...], cotp_s[...], (((0,), (0,)), ((), ())),
                               preferred_element_type=F32)
    for b in range(16):
        piece = temporal[b * 32:(b + 1) * 32]
        keep_ref[b, 144:, :] = piece[:, :128]
        send_ref[b, 144:, :] = piece[:, 128:].astype(BF)
    for copy in copies:
        copy.wait()
    for tap in range(TAPS):
        put(tap * C, jnp.dot(patcht_s[tap * C:(tap + 1) * C, :], gpre_s[...],
                             preferred_element_type=F32))
    output.wait()


def make_patches(flags, plan, tiles, cotangent, pick, marks):
    hbm = pl.BlockSpec(memory_space=pltpu.HBM)
    vmem = pl.BlockSpec(memory_space=pltpu.VMEM)
    smem = pl.BlockSpec(memory_space=pltpu.SMEM)
    return pl.pallas_call(
        patch_kernel,
        in_specs=[smem, smem, hbm, vmem, vmem, vmem],
        out_specs=[vmem, hbm, hbm, vmem],
        out_shape=[
            jax.ShapeDtypeStruct((GROUP_ROWS, TAPS * C), BF),
            pltpu.HBM((REST_ROWS, TAPS * C), BF),
            pltpu.HBM((TAPS * C, ROWS), BF),
            jax.ShapeDtypeStruct((COT_ROWS, C), BF),
        ],
        scratch_shapes=[
            pltpu.VMEM((OWNED, IN_PIX, C), BF),
            pltpu.VMEM((REST_ROWS, TAPS * C), BF),
            pltpu.VMEM((TAPS * C, ROWS), BF),
            pltpu.SemaphoreType.DMA((STEPS,)),
            pltpu.SemaphoreType.DMA((2 * STEPS,)),
        ],
        compiler_params=pltpu.CompilerParams(vmem_limit_bytes=32 * 2**20),
        cost_estimate=pl.CostEstimate(flops=6 * 10**9, bytes_accessed=15 * 10**6, transcendentals=0),
        name="patches",
    )(flags, plan, pltpu.with_memory_space_constraint(tiles, pltpu.HBM), cotangent, pick, marks)


def run_section(core, plan, got, other, cot_live, perm, patches, patches_t):
    hbm = pl.BlockSpec(memory_space=pltpu.HBM)
    vmem = pl.BlockSpec(memory_space=pltpu.VMEM)
    smem = pl.BlockSpec(memory_space=pltpu.SMEM)
    return pl.pallas_call(
        main_kernel,
        in_specs=[smem] * 2 + [vmem] * 5 + [hbm],
        out_specs=[hbm, vmem, vmem],
        out_shape=[
            pltpu.HBM((OWNED, OUT_PIX, C), BF),
            jax.ShapeDtypeStruct((16, 176, 128), F32),
            jax.ShapeDtypeStruct((16, 176, 128), BF),
        ],
        scratch_shapes=[
            pltpu.VMEM((OWNED, OUT_PIX, C), BF),
            pltpu.VMEM((TAPS * C, ROWS), BF),
            pltpu.VMEM((TAPS * C, C), BF),
            pltpu.VMEM((2 * C, C), BF),
            pltpu.VMEM((COT_ROWS, 2 * C), BF),
            pltpu.VMEM((ROWS, C), BF),
            pltpu.VMEM((COT_ROWS, C), BF),
            pltpu.SemaphoreType.DMA((TAPS + 1,)),
        ],
        compiler_params=pltpu.CompilerParams(vmem_limit_bytes=36 * 2**20),
        cost_estimate=pl.CostEstimate(flops=4 * 10**9, bytes_accessed=15 * 10**6, transcendentals=0),
        name="section",
    )(core, plan, got, other, cot_live, perm, patches,
      pltpu.with_memory_space_constraint(patches_t, pltpu.HBM))


def spread_kernel(core_ref, spatial_hbm, temporal_hbm, out_ref, rows_s, sems):
    reads = [pltpu.make_async_copy(spatial_hbm, rows_s.at[pl.ds(0, 144)], sems.at[0]),
             pltpu.make_async_copy(temporal_hbm, rows_s.at[pl.ds(144, 32)], sems.at[1])]
    for copy in reads:
        copy.start()
    for copy in reads:
        copy.wait()

    def write(first):
        mine = rows_s[first:first + SHARE, :]
        for b in range(16):
            out_ref[b] = mine

    @pl.when(core_ref[0] == 0)
    def _():
        write(0)

    @pl.when(core_ref[0] != 0)
    def _():
        write(176 - SHARE)


def spread(core, spatial, temporal):
    smem = pl.BlockSpec(memory_space=pltpu.SMEM)
    hbm = pl.BlockSpec(memory_space=pltpu.HBM)
    return pl.pallas_call(
        spread_kernel,
        in_specs=[smem, hbm, hbm],
        out_specs=pl.BlockSpec(memory_space=pltpu.VMEM),
        out_shape=jax.ShapeDtypeStruct((16, SHARE, C), BF),
        scratch_shapes=[
            pltpu.VMEM((176, C), BF),
            pltpu.SemaphoreType.DMA((2,)),
        ],
        compiler_params=pltpu.CompilerParams(vmem_limit_bytes=8 * 2**20),
        name="spread",
    )(core, pltpu.with_memory_space_constraint(spatial, pltpu.HBM),
      pltpu.with_memory_space_constraint(temporal, pltpu.HBM))


def finish_kernel(part_ref, spatial_hbm, temporal_hbm, spatial_s, temporal_s, sems):
    total = part_ref[0]
    for z in range(1, part_ref.shape[0]):
        total = total + part_ref[z]
    total = total * FACTOR
    spatial_s[...] = total[:, :144]
    temporal_s[...] = total[:, 144:]
    copies = [pltpu.make_async_copy(spatial_s, spatial_hbm, sems.at[0]),
              pltpu.make_async_copy(temporal_s, temporal_hbm, sems.at[1])]
    for copy in copies:
        copy.start()
    for copy in copies:
        copy.wait()


def finish(part):
    hbm = pl.BlockSpec(memory_space=pltpu.HBM)
    return pl.pallas_call(
        finish_kernel,
        in_specs=[pl.BlockSpec(memory_space=pltpu.VMEM)],
        out_specs=[hbm, hbm],
        out_shape=[pltpu.HBM((8, 144), F32), pltpu.HBM((8, 32), F32)],
        scratch_shapes=[
            pltpu.VMEM((8, 144), F32),
            pltpu.VMEM((8, 32), F32),
            pltpu.SemaphoreType.DMA((2,)),
        ],
        compiler_params=pltpu.CompilerParams(vmem_limit_bytes=4 * 2**20),
        name="finish",
    )(part)


def permutation(core):
    row = lax.broadcasted_iota(jnp.int32, (C, C), 0)
    col = lax.broadcasted_iota(jnp.int32, (C, C), 1)
    wanted = ((col % 128) // 8) * 16 + jnp.bitwise_xor(core, col // 128) * 8 + col % 8
    return (row == wanted).astype(BF)


def per_device(tiles, cotangent, halo_flags, send_plan, spatial_weight, temporal_weight):
    core = lax.axis_index("dp") % 2
    siblings = [(i, i ^ 1) for i in range(32)]
    core_id = core.reshape(1).astype(jnp.int32)
    got = lax.all_to_all(spread(core_id, spatial_weight, temporal_weight), "bal", 0, 0)

    pick, marks = selection()
    perm = permutation(core)
    flags = halo_flags.T
    plan = send_plan[0].T
    first, patches, patches_t, cot_live = make_patches(
        flags, plan, tiles, cotangent, pick, marks
    )
    got, patches, patches_t = lax.optimization_barrier((got, patches, patches_t))
    other = lax.ppermute(got, "dp", siblings)
    features, keep, send = run_section(
        core_id, plan, got, other, cot_live, perm, fetch(first, patches), patches_t
    )

    theirs = lax.ppermute(send, "dp", siblings)
    chip = (keep + theirs.astype(F32)).astype(BF)
    part = lax.all_to_all(chip, "bal", 0, 0)
    part = jnp.sum(part.astype(F32), axis=0)
    part = part.T.reshape(16, 8, 176)
    along_z = [[2 * z + c for z in range(16)] for c in range(2)]
    last = lax.all_to_all(part, "dp", 0, 0, axis_index_groups=along_z)
    spatial_t, temporal_t = finish(last)
    return features, spatial_t.T, temporal_t.T


def solution(mesh):
    in_specs = (
        P(("dp", "bal"), None, None),
        P(("dp", "bal"), None, None),
        P(("dp", "bal"), None),
        P(("dp", "bal"), None, None),
        P("bal", None),
        P("bal", None),
    )
    out_specs = (P(("dp", "bal"), None, None), P("bal", "dp"), P("bal", "dp"))
    return jax.shard_map(
        per_device, mesh=mesh, in_specs=in_specs, out_specs=out_specs, check_vma=False
    )
```
